32 devices in a mesh: rep: 4 (over x, core), fsdp: 8 (over z, y).
Axes of the slice: x: 2, y: 2, z: 4, core: 2. Of those that a mesh axis runs over, the one named last changes fastest.
Arguments:
- base_params: bfloat16 [14336, 8192], P(None, 'fsdp'), may hold values from -6 to 6
- local_params: bfloat16 [4, 14336, 8192], P('rep', None, 'fsdp'), may hold values from -6 to 6
- momentum: float32 [14336, 8192], P(('rep', 'fsdp')), may hold values from -4 to 4
Outputs:
- new_params: bfloat16 [14336, 8192], P(None, 'fsdp')
The draws below stay inside these ranges and needn't reach their ends.
All inputs are finite; a program needn't handle non-finite values.
Results may differ from the reference program's by a relative error of at most 0.0077.
Values may be sent and summed in bfloat16 or wider, within the bound.
A program may use at most 512 MiB of HBM per device.

```python
import jax
import jax.numpy as jnp
from jax import lax

D = 8192
FF = 14336
ROWS_OWN = 448
REPS = 4
N_REP = 4


def levels(own_key, extent, shards, low, top_value):
    def one(axis_at, blocks):
        draws = jax.random.uniform(jax.random.fold_in(jax.random.fold_in(own_key, 6), axis_at), (blocks,), jnp.float32, low / len(shards), top_value / len(shards))
        return jnp.repeat(jnp.exp(draws), extent[axis_at] // blocks).reshape((-1,) + (1,) * (len(extent) - axis_at - 1))

    factor_of = one(*shards[0])
    for cut in shards[1:]:
        factor_of = factor_of * one(*cut)
    return factor_of


def normal_values(own_key, shape, spread, limit, shards=(), kind=jnp.bfloat16):
    factor_of = levels(own_key, shape, shards, -0.22, 0.18) if shards else 1.0
    array = jax.random.normal(own_key, shape, jnp.float32) * spread * factor_of
    return jnp.minimum(jnp.maximum(array, -limit), limit).astype(kind)


def setup_inputs(seed: int = 0) -> dict:
    key_list = jax.random.split(jax.random.key(seed), 4)
    base_params = normal_values(key_list[0], (FF, D), 1.0, 6.0, ((1, 8),))
    local_params = normal_values(key_list[1], (REPS, FF, D), 1.0, 6.0, ((0, 4), (2, 8)))
    momentum = normal_values(key_list[2], (FF, D), 0.5, 4.0, ((0, 32),), jnp.float32)
    return dict(base_params=base_params, local_params=local_params, momentum=momentum)


epsilon = 1e-6
code_max = 448.0
outer_rate = 0.7
nesterov = 0.9


def block_encode(tensor):
    dims = tensor.shape
    blocks = tensor.reshape(dims[:-1] + (dims[-1] // 128, 128))
    largest = jnp.max(jnp.abs(blocks), axis=-1)
    scales = ((largest + epsilon) / code_max).astype(jnp.bfloat16)
    scales = lax.optimization_barrier(scales)
    symbols = (blocks / scales.astype(jnp.float32)[..., None]).astype(jnp.bfloat16)
    return symbols.reshape(dims), scales


def block_decode(symbols, scales):
    dims = symbols.shape
    blocks = symbols.astype(jnp.float32).reshape(dims[:-1] + (dims[-1] // 128, 128))
    return (blocks * scales.astype(jnp.float32)[..., None]).reshape(dims)


def reference(base_params, local_params, momentum):
    block_count = FF // ROWS_OWN
    base_blocks = base_params.reshape(block_count, ROWS_OWN, D)
    local_blocks = jnp.swapaxes(local_params.reshape(N_REP, block_count, ROWS_OWN, D), 0, 1)
    moment_blocks = momentum.reshape(block_count, ROWS_OWN, D)

    def one_block(items):
        base_rows, local_rows, moment_rows = items
        start = base_rows.astype(jnp.float32)
        total = jnp.zeros((ROWS_OWN, D), jnp.float32)
        for replica in range(N_REP):
            symbols, scales = lax.optimization_barrier(block_encode(start - local_rows[replica].astype(jnp.float32)))
            total = total + block_decode(symbols, scales)
        outer_grad = total / N_REP
        moment_next = nesterov * moment_rows + outer_grad
        update = outer_rate * (outer_grad + nesterov * moment_next)
        symbols, scales = lax.optimization_barrier(block_encode(update))
        return (start - block_decode(symbols, scales)).astype(jnp.bfloat16)

    return lax.map(one_block, (base_blocks, local_blocks, moment_blocks)).reshape(FF, D)
```

```python
import functools

import jax
import jax.numpy as jnp
from jax import lax
from jax.experimental import pallas as pl
from jax.experimental.pallas import tpu as pltpu
from jax.sharding import PartitionSpec as P

epsilon = 1e-06
code_max = 448.0
outer_rate = 0.7
nesterov = 0.9

BLOCK = 128
GROUP = 16
MESH = pl.DeviceIdType.MESH

LAG_PAIR = 1
LAG_OWN = 4
LAG_PASS = 7
SLOTS = 4


def round_trip(values):
    largest = jnp.max(jnp.abs(values), axis=-1, keepdims=True)
    scales = ((largest + epsilon) / code_max).astype(jnp.bfloat16).astype(jnp.float32)
    symbols = (values * (1.0 / scales)).astype(jnp.bfloat16)
    return symbols.astype(jnp.float32) * scales


def kernel(
    rep_count, fsdp_count, chunk, base, loc, mom, out,
    base_buf, loc_buf, mom_buf, mom_out, sib_out, pair_out, new_out,
    sib_in, pair_in, mom_in,
    base_sem, loc_sem, mom_sem,
    mom_send, sib_send, pair_send, new_send, pass_send,
    sib_recv, pair_recv, mom_recv, new_recv, far_recv,
):
    r = lax.axis_index("rep")
    f = lax.axis_index("fsdp")
    x = lax.div(r, 2)
    c = lax.rem(r, 2)
    sibling = (2 * x + 1 - c, f)
    across = (2 * (1 - x) + c, f)
    cols = base.shape[1]
    quarter_rows = base.shape[0] // rep_count
    own_rows = mom.shape[0]
    per_piece = own_rows // chunk
    chunks = quarter_rows // chunk
    quarters = (2 * (1 - x) + 1 - c, 2 * x + 1 - c, 2 * (1 - x) + c, 2 * x + c)
    lags = (0, 0, LAG_PAIR, LAG_OWN)

    barrier = pltpu.get_barrier_semaphore()
    pl.semaphore_signal(barrier, inc=1, device_id=sibling, device_id_type=MESH)
    pl.semaphore_signal(barrier, inc=1, device_id=across, device_id_type=MESH)

    def greet(j, carry):
        peer = lax.rem(f + j, fsdp_count)
        pl.semaphore_signal(barrier, inc=1, device_id=(r, peer), device_id_type=MESH)
        return carry

    lax.fori_loop(1, fsdp_count, greet, 0)

    def rows_of(k, quarter):
        piece = lax.rem(f + lax.div(k, per_piece), fsdp_count)
        start = quarter * quarter_rows + piece * own_rows + lax.rem(k, per_piece) * chunk
        return pl.ds(pl.multiple_of(start, 16), chunk)

    def mom_peer(k):
        return lax.rem(f + fsdp_count - lax.div(k, per_piece), fsdp_count)

    def loads(i, k):
        slot = lax.rem(k, 2)
        rows = rows_of(k, quarters[i])
        return (
            pltpu.make_async_copy(base.at[rows, :], base_buf.at[slot, i], base_sem.at[slot, i]),
            pltpu.make_async_copy(loc.at[0, rows, :], loc_buf.at[slot, i], loc_sem.at[slot, i]),
        )

    def mom_load(k):
        slot = lax.rem(k, 2)
        start = pl.multiple_of(lax.rem(k, per_piece) * chunk, 16)
        first = pl.multiple_of(mom_peer(k) * cols, BLOCK)
        return pltpu.make_async_copy(
            mom.at[pl.ds(start, chunk), pl.ds(first, cols)], mom_buf.at[slot], mom_sem.at[slot]
        )

    def remote(src, dst, send, recv, device):
        return pltpu.make_async_remote_copy(
            src_ref=src, dst_ref=dst, send_sem=send, recv_sem=recv,
            device_id=device, device_id_type=MESH,
        )

    def mom_copy(k):
        slot = lax.rem(k, SLOTS)
        return remote(
            mom_out.at[slot], mom_in.at[k], mom_send.at[slot], mom_recv.at[k], (r, mom_peer(k))
        )

    def sib_copy(i, k):
        slot = lax.rem(k, SLOTS)
        return remote(
            sib_out.at[slot, i], sib_in.at[k, i], sib_send.at[slot, i], sib_recv.at[k, i], sibling
        )

    def pair_copy(k):
        slot = lax.rem(k, SLOTS)
        return remote(
            pair_out.at[slot], pair_in.at[k], pair_send.at[slot], pair_recv.at[k], across
        )

    def new_copies(k):
        slot = lax.rem(k, SLOTS)
        src = new_out.at[slot]
        dst = out.at[rows_of(k, quarters[3]), :]
        return (
            remote(src, dst, new_send.at[slot, 0], new_recv.at[k], across),
            remote(src, dst, new_send.at[slot, 1], far_recv.at[0], sibling),
            pltpu.make_async_copy(src, dst, new_send.at[slot, 2]),
        )

    def pass_copy(rows):
        return remote(out.at[rows, :], out.at[rows, :], pass_send, far_recv.at[1], sibling)

    def active(k):
        return jnp.logical_and(k >= 0, k < chunks)

    def prefetch(step):
        @pl.when(active(step))
        def _():
            mom_load(step).start()

        for i in range(4):
            k = step - lags[i]

            @pl.when(active(k))
            def _(i=i, k=k):
                for copy in loads(i, k):
                    copy.start()

    def each_block(body):
        def group(g, carry):
            rows = pl.ds(pl.multiple_of(g * GROUP, GROUP), GROUP)
            for b in range(cols // BLOCK):
                body(rows, pl.ds(b * BLOCK, BLOCK))
            return carry

        lax.fori_loop(0, chunk // GROUP, group, 0)

    def change(i, slot, rows, block):
        start = base_buf[slot, i, rows, block].astype(jnp.float32)
        return start, round_trip(start - loc_buf[slot, i, rows, block].astype(jnp.float32))

    def send_momentum(k):
        slot = lax.rem(k, 2)
        mom_load(k).wait()

        @pl.when(k < per_piece)
        def _():
            def body(rows, block):
                mom_in[k, rows, block] = mom_buf[slot, rows, block].astype(jnp.bfloat16)

            each_block(body)

        @pl.when(k >= per_piece)
        def _():
            @pl.when(k >= per_piece + SLOTS)
            def _():
                mom_copy(k - SLOTS).wait_send()

            to = lax.rem(k, SLOTS)

            def body(rows, block):
                mom_out[to, rows, block] = mom_buf[slot, rows, block].astype(jnp.bfloat16)

            each_block(body)
            mom_copy(k).start()

    def send_sibling(k):
        slot = lax.rem(k, 2)
        to = lax.rem(k, SLOTS)
        for i in range(2):
            for copy in loads(i, k):
                copy.wait()

            @pl.when(k >= SLOTS)
            def _(i=i):
                sib_copy(i, k - SLOTS).wait_send()

            def body(rows, block, i=i):
                sib_out[to, i, rows, block] = change(i, slot, rows, block)[1].astype(jnp.bfloat16)

            each_block(body)
            sib_copy(i, k).start()

    def send_pair(k):
        slot = lax.rem(k, 2)
        to = lax.rem(k, SLOTS)
        for copy in loads(2, k):
            copy.wait()

        @pl.when(k >= SLOTS)
        def _():
            pair_copy(k - SLOTS).wait_send()

        sib_copy(0, k).wait_recv()

        def body(rows, block):
            total = change(2, slot, rows, block)[1] + sib_in[k, 0, rows, block].astype(jnp.float32)
            pair_out[to, rows, block] = total.astype(jnp.bfloat16)

        each_block(body)
        pair_copy(k).start()

    def step_own(k):
        slot = lax.rem(k, 2)
        to = lax.rem(k, SLOTS)
        for copy in loads(3, k):
            copy.wait()

        @pl.when(k >= SLOTS)
        def _():
            first, second, third = new_copies(k - SLOTS)
            first.wait_send()
            second.wait_send()
            third.wait()

        sib_copy(1, k).wait_recv()

        @pl.when(k >= per_piece)
        def _():
            mom_copy(k).wait_recv()

        pair_copy(k).wait_recv()

        def body(rows, block):
            start, mine = change(3, slot, rows, block)
            total = mine + sib_in[k, 1, rows, block].astype(jnp.float32)
            total = total + pair_in[k, rows, block].astype(jnp.float32)
            outer_grad = total / rep_count
            moment_next = nesterov * mom_in[k, rows, block].astype(jnp.float32) + outer_grad
            update = outer_rate * (outer_grad + nesterov * moment_next)
            new_out[to, rows, block] = (start - round_trip(update)).astype(jnp.bfloat16)

        each_block(body)
        for copy in new_copies(k):
            copy.start()

    def pass_on(k):
        rows = rows_of(k, quarters[2])
        remote(
            out.at[rows, :], out.at[rows, :], pass_send, new_recv.at[k], across
        ).wait_recv()
        pass_copy(rows).start()

    prefetch(0)
    pl.semaphore_wait(barrier, fsdp_count + 1)

    def step(s, carry):
        prefetch(s + 1)
        for lag, stage in (
            (0, send_sibling),
            (LAG_PAIR, send_pair),
            (0, send_momentum),
            (LAG_OWN, step_own),
            (LAG_PASS, pass_on),
        ):
            k = s - lag

            @pl.when(active(k))
            def _(stage=stage, k=k):
                stage(k)

        return carry

    lax.fori_loop(0, chunks + LAG_PASS, step, 0)

    def drain(k, carry):
        mom_copy(k).wait_send()
        sib_copy(0, k).wait_send()
        sib_copy(1, k).wait_send()
        pair_copy(k).wait_send()
        first, second, third = new_copies(k)
        first.wait_send()
        second.wait_send()
        third.wait()
        return carry

    lax.fori_loop(chunks - SLOTS, chunks, drain, 0)

    def quarter_of(index):
        return pl.ds(pl.multiple_of(index * quarter_rows, 16), quarter_rows)

    pass_copy(quarter_of(quarters[2])).wait_send()
    for i in range(2):
        rows = quarter_of(quarters[1 - i])
        remote(out.at[rows, :], out.at[rows, :], pass_send, far_recv.at[i], sibling).wait_recv()


def chunk_rows(own_rows):
    best = GROUP
    for size in range(GROUP, 113, GROUP):
        if own_rows % size == 0:
            best = size
    return best


def local(base_params, local_params, momentum):
    rep_count = lax.axis_size("rep")
    fsdp_count = lax.axis_size("fsdp")
    total_rows, cols = base_params.shape
    chunk = chunk_rows(momentum.shape[0])
    chunks = total_rows // rep_count // chunk
    bf16, f32 = jnp.bfloat16, jnp.float32
    dma = pltpu.SemaphoreType.DMA
    anywhere = pl.BlockSpec(memory_space=pl.ANY)
    return pl.pallas_call(
        functools.partial(kernel, rep_count, fsdp_count, chunk),
        out_shape=jax.ShapeDtypeStruct((total_rows, cols), bf16),
        in_specs=[anywhere] * 3,
        out_specs=anywhere,
        scratch_shapes=[
            pltpu.VMEM((2, 4, chunk, cols), bf16),
            pltpu.VMEM((2, 4, chunk, cols), bf16),
            pltpu.VMEM((2, chunk, cols), f32),
            pltpu.VMEM((SLOTS, chunk, cols), bf16),
            pltpu.VMEM((SLOTS, 2, chunk, cols), bf16),
            pltpu.VMEM((SLOTS, chunk, cols), bf16),
            pltpu.VMEM((SLOTS, chunk, cols), bf16),
            pltpu.VMEM((chunks, 2, chunk, cols), bf16),
            pltpu.VMEM((chunks, chunk, cols), bf16),
            pltpu.VMEM((chunks, chunk, cols), bf16),
            dma((2, 4)),
            dma((2, 4)),
            dma((2,)),
            dma((SLOTS,)),
            dma((SLOTS, 2)),
            dma((SLOTS,)),
            dma((SLOTS, 3)),
            dma,
            dma((chunks, 2)),
            dma((chunks,)),
            dma((chunks,)),
            dma((chunks,)),
            dma((2,)),
        ],
        compiler_params=pltpu.CompilerParams(
            collective_id=0, has_side_effects=True, vmem_limit_bytes=56 * 1024 * 1024
        ),
    )(base_params, local_params, momentum)


def solution(mesh):
    return jax.shard_map(
        local,
        mesh=mesh,
        in_specs=(P(None, "fsdp"), P("rep", None, "fsdp"), P(("rep", "fsdp"), None)),
        out_specs=P(None, "fsdp"),
        check_vma=False,
    )
```

```python
import functools

import jax
import jax.numpy as jnp
from jax import lax
from jax.experimental import pallas as pl
from jax.experimental.pallas import tpu as pltpu
from jax.sharding import PartitionSpec as P

epsilon = 1e-06
code_max = 448.0
outer_rate = 0.7
nesterov = 0.9

BLOCK = 128
GROUP = 16
MESH = pl.DeviceIdType.MESH

LAG_PAIR = 1
LAG_OWN = 4
LAG_PASS = 7
SLOTS = 4
PARTS = 8
RING = 10


def round_trip(values):
    largest = jnp.max(jnp.abs(values), axis=-1, keepdims=True)
    scales = ((largest + epsilon) / code_max).astype(jnp.bfloat16).astype(jnp.float32)
    symbols = (values * (1.0 / scales)).astype(jnp.bfloat16)
    return symbols.astype(jnp.float32) * scales


def kernel(
    rep_count, fsdp_count, chunk, base, loc, mom, out,
    base_buf, loc_buf, mom_buf, mom_out, sib_out, pair_out, new_out,
    sib_in, pair_in, mom_in,
    base_sem, loc_sem, mom_sem,
    mom_send, sib_send, pair_send, new_send, pass_send,
    sib_recv, pair_recv, mom_recv, new_recv, far_recv, sib_free, pair_free,
):
    r = lax.axis_index("rep")
    f = lax.axis_index("fsdp")
    x = lax.div(r, 2)
    c = lax.rem(r, 2)
    sibling = (2 * x + 1 - c, f)
    across = (2 * (1 - x) + c, f)
    cols = base.shape[1]
    quarter_rows = base.shape[0] // rep_count
    own_rows = mom.shape[0]
    per_piece = own_rows // chunk
    chunks = quarter_rows // chunk
    quarters = (2 * (1 - x) + 1 - c, 2 * x + 1 - c, 2 * (1 - x) + c, 2 * x + c)
    lags = (0, 0, LAG_PAIR, LAG_OWN)

    barrier = pltpu.get_barrier_semaphore()
    pl.semaphore_signal(barrier, inc=1, device_id=sibling, device_id_type=MESH)
    pl.semaphore_signal(barrier, inc=1, device_id=across, device_id_type=MESH)

    def greet(j, carry):
        peer = lax.rem(f + j, fsdp_count)
        pl.semaphore_signal(barrier, inc=1, device_id=(r, peer), device_id_type=MESH)
        return carry

    lax.fori_loop(1, fsdp_count, greet, 0)

    def rows_of(k, quarter):
        piece = lax.rem(f + lax.div(k, per_piece), fsdp_count)
        start = quarter * quarter_rows + piece * own_rows + lax.rem(k, per_piece) * chunk
        return pl.ds(pl.multiple_of(start, 16), chunk)

    def mom_peer(k):
        return lax.rem(f + fsdp_count - lax.div(k, per_piece), fsdp_count)

    def loads(i, k):
        slot = lax.rem(k, 2)
        rows = rows_of(k, quarters[i])
        return (
            pltpu.make_async_copy(base.at[rows, :], base_buf.at[slot, i], base_sem.at[slot, i]),
            pltpu.make_async_copy(loc.at[0, rows, :], loc_buf.at[slot, i], loc_sem.at[slot, i]),
        )

    def mom_load(k):
        slot = lax.rem(k, 2)
        start = pl.multiple_of(lax.rem(k, per_piece) * chunk, 16)
        first = pl.multiple_of(mom_peer(k) * cols, BLOCK)
        return pltpu.make_async_copy(
            mom.at[pl.ds(start, chunk), pl.ds(first, cols)], mom_buf.at[slot], mom_sem.at[slot]
        )

    def remote(src, dst, send, recv, device):
        return pltpu.make_async_remote_copy(
            src_ref=src, dst_ref=dst, send_sem=send, recv_sem=recv,
            device_id=device, device_id_type=MESH,
        )

    def mom_copy(k):
        slot = lax.rem(k, SLOTS)
        return remote(
            mom_out.at[slot], mom_in.at[k], mom_send.at[slot], mom_recv.at[k], (r, mom_peer(k))
        )

    def sib_copy(i, k):
        slot = lax.rem(k, SLOTS)
        return remote(
            sib_out.at[slot, i], sib_in.at[lax.rem(k, RING), i], sib_send.at[slot, i],
            sib_recv.at[lax.rem(k, RING), i], sibling,
        )

    def pair_copy(k):
        slot = lax.rem(k, SLOTS)
        return remote(
            pair_out.at[slot], pair_in.at[lax.rem(k, RING)], pair_send.at[slot],
            pair_recv.at[lax.rem(k, RING)], across,
        )

    def new_copies(k):
        slot = lax.rem(k, SLOTS)
        src = new_out.at[slot]
        dst = out.at[rows_of(k, quarters[3]), :]
        return (
            remote(src, dst, new_send.at[slot, 0], new_recv.at[k], across),
            remote(src, dst, new_send.at[slot, 1], far_recv.at[0], sibling),
            pltpu.make_async_copy(src, dst, new_send.at[slot, 2]),
        )

    def pass_copy(rows):
        return remote(out.at[rows, :], out.at[rows, :], pass_send, far_recv.at[1], sibling)

    def active(k):
        return jnp.logical_and(k >= 0, k < chunks)

    def prefetch(step):
        @pl.when(active(step))
        def _():
            mom_load(step).start()

        for i in range(4):
            k = step - lags[i]

            @pl.when(active(k))
            def _(i=i, k=k):
                for copy in loads(i, k):
                    copy.start()

    def each_block(body):
        def group(g, carry):
            rows = pl.ds(pl.multiple_of(g * GROUP, GROUP), GROUP)
            for b in range(cols // BLOCK):
                body(rows, pl.ds(b * BLOCK, BLOCK))
            return carry

        lax.fori_loop(0, chunk // GROUP, group, 0)

    def change(i, slot, rows, block):
        start = base_buf[slot, i, rows, block].astype(jnp.float32)
        return start, round_trip(start - loc_buf[slot, i, rows, block].astype(jnp.float32))

    def send_momentum(k):
        slot = lax.rem(k, 2)
        mom_load(k).wait()

        @pl.when(k < per_piece)
        def _():
            def body(rows, block):
                mom_in[k, rows, block] = mom_buf[slot, rows, block].astype(jnp.bfloat16)

            each_block(body)

        @pl.when(k >= per_piece)
        def _():
            @pl.when(k >= per_piece + SLOTS)
            def _():
                mom_copy(k - SLOTS).wait_send()

            to = lax.rem(k, SLOTS)

            def body(rows, block):
                mom_out[to, rows, block] = mom_buf[slot, rows, block].astype(jnp.bfloat16)

            each_block(body)
            mom_copy(k).start()

    def send_sibling(k):
        slot = lax.rem(k, 2)
        to = lax.rem(k, SLOTS)

        @pl.when(k >= RING)
        def _():
            pl.semaphore_wait(sib_free, 1)

        for i in range(2):
            for copy in loads(i, k):
                copy.wait()

            @pl.when(k >= SLOTS)
            def _(i=i):
                sib_copy(i, k - SLOTS).wait_send()

            def body(rows, block, i=i):
                sib_out[to, i, rows, block] = change(i, slot, rows, block)[1].astype(jnp.bfloat16)

            each_block(body)
            sib_copy(i, k).start()

    def send_pair(k):
        slot = lax.rem(k, 2)
        to = lax.rem(k, SLOTS)
        for copy in loads(2, k):
            copy.wait()

        @pl.when(k >= SLOTS)
        def _():
            pair_copy(k - SLOTS).wait_send()

        @pl.when(k >= RING)
        def _():
            pl.semaphore_wait(pair_free, 1)

        sib_copy(0, k).wait_recv()

        def body(rows, block):
            total = change(2, slot, rows, block)[1] + sib_in[lax.rem(k, RING), 0, rows, block].astype(jnp.float32)
            pair_out[to, rows, block] = total.astype(jnp.bfloat16)

        each_block(body)
        pair_copy(k).start()

    def step_own(k):
        slot = lax.rem(k, 2)
        to = lax.rem(k, SLOTS)
        for copy in loads(3, k):
            copy.wait()

        @pl.when(k >= SLOTS)
        def _():
            first, second, third = new_copies(k - SLOTS)
            first.wait_send()
            second.wait_send()
            third.wait()

        sib_copy(1, k).wait_recv()

        @pl.when(k >= per_piece)
        def _():
            mom_copy(k).wait_recv()

        pair_copy(k).wait_recv()

        def body(rows, block):
            start, mine = change(3, slot, rows, block)
            total = mine + sib_in[lax.rem(k, RING), 1, rows, block].astype(jnp.float32)
            total = total + pair_in[lax.rem(k, RING), rows, block].astype(jnp.float32)
            outer_grad = total / rep_count
            moment_next = nesterov * mom_in[k, rows, block].astype(jnp.float32) + outer_grad
            update = outer_rate * (outer_grad + nesterov * moment_next)
            new_out[to, rows, block] = (start - round_trip(update)).astype(jnp.bfloat16)

        each_block(body)
        for copy in new_copies(k):
            copy.start()

        @pl.when(k < chunks - RING)
        def _():
            pl.semaphore_signal(sib_free, inc=1, device_id=sibling, device_id_type=MESH)
            pl.semaphore_signal(pair_free, inc=1, device_id=across, device_id_type=MESH)

    def pass_on(k):
        rows = rows_of(k, quarters[2])
        remote(
            out.at[rows, :], out.at[rows, :], pass_send, new_recv.at[k], across
        ).wait_recv()
        pass_copy(rows).start()

    prefetch(0)
    pl.semaphore_wait(barrier, fsdp_count + 1)

    def step(s, carry):
        prefetch(s + 1)
        for lag, stage in (
            (0, send_sibling),
            (LAG_PAIR, send_pair),
            (0, send_momentum),
            (LAG_OWN, step_own),
            (LAG_PASS, pass_on),
        ):
            k = s - lag

            @pl.when(active(k))
            def _(stage=stage, k=k):
                stage(k)

        return carry

    lax.fori_loop(0, chunks + LAG_PASS, step, 0)

    def drain(k, carry):
        mom_copy(k).wait_send()
        sib_copy(0, k).wait_send()
        sib_copy(1, k).wait_send()
        pair_copy(k).wait_send()
        first, second, third = new_copies(k)
        first.wait_send()
        second.wait_send()
        third.wait()
        return carry

    lax.fori_loop(chunks - SLOTS, chunks, drain, 0)

    def quarter_of(index):
        return pl.ds(pl.multiple_of(index * quarter_rows, 16), quarter_rows)

    pass_copy(quarter_of(quarters[2])).wait_send()
    for i in range(2):
        rows = quarter_of(quarters[1 - i])
        remote(out.at[rows, :], out.at[rows, :], pass_send, far_recv.at[i], sibling).wait_recv()


def write_kernel(rows, src, dst, sem):
    copies = [
        pltpu.make_async_copy(
            src.at[pl.ds(p * rows, rows), :], dst.at[pl.ds(p * rows, rows), :], sem.at[p]
        )
        for p in range(PARTS)
    ]
    for copy in copies:
        copy.start()
    for copy in copies:
        copy.wait()


def chunk_rows(own_rows):
    for size in (64, 80, 96, 112, 128, 48, 32):
        if own_rows % size == 0:
            return size
    return GROUP


def local(base_params, local_params, momentum):
    rep_count = lax.axis_size("rep")
    fsdp_count = lax.axis_size("fsdp")
    total_rows, cols = base_params.shape
    chunk = chunk_rows(momentum.shape[0])
    chunks = total_rows // rep_count // chunk
    bf16, f32 = jnp.bfloat16, jnp.float32
    dma = pltpu.SemaphoreType.DMA
    anywhere = pl.BlockSpec(memory_space=pl.ANY)
    gathered = pl.pallas_call(
        functools.partial(kernel, rep_count, fsdp_count, chunk),
        out_shape=pltpu.VMEM((total_rows, cols), bf16),
        in_specs=[anywhere] * 3,
        out_specs=anywhere,
        scratch_shapes=[
            pltpu.VMEM((2, 4, chunk, cols), bf16),
            pltpu.VMEM((2, 4, chunk, cols), bf16),
            pltpu.VMEM((2, chunk, cols), f32),
            pltpu.VMEM((SLOTS, chunk, cols), bf16),
            pltpu.VMEM((SLOTS, 2, chunk, cols), bf16),
            pltpu.VMEM((SLOTS, chunk, cols), bf16),
            pltpu.VMEM((SLOTS, chunk, cols), bf16),
            pltpu.VMEM((RING, 2, chunk, cols), bf16),
            pltpu.VMEM((RING, chunk, cols), bf16),
            pltpu.VMEM((chunks, chunk, cols), bf16),
            dma((2, 4)),
            dma((2, 4)),
            dma((2,)),
            dma((SLOTS,)),
            dma((SLOTS, 2)),
            dma((SLOTS,)),
            dma((SLOTS, 3)),
            dma,
            dma((RING, 2)),
            dma((RING,)),
            dma((chunks,)),
            dma((chunks,)),
            dma((2,)),
            pltpu.SemaphoreType.REGULAR,
            pltpu.SemaphoreType.REGULAR,
        ],
        compiler_params=pltpu.CompilerParams(
            collective_id=0, has_side_effects=True, vmem_limit_bytes=24 * 1024 * 1024
        ),
    )(base_params, local_params, momentum)
    return pl.pallas_call(
        functools.partial(write_kernel, total_rows // PARTS),
        out_shape=jax.ShapeDtypeStruct((total_rows, cols), bf16),
        in_specs=[anywhere],
        out_specs=anywhere,
        scratch_shapes=[dma((PARTS,))],
        compiler_params=pltpu.CompilerParams(vmem_limit_bytes=1024 * 1024),
    )(gathered)


def solution(mesh):
    return jax.shard_map(
        local,
        mesh=mesh,
        in_specs=(P(None, "fsdp"), P("rep", None, "fsdp"), P(("rep", "fsdp"), None)),
        out_specs=P(None, "fsdp"),
        check_vma=False,
    )
```

```python
import functools

import jax
import jax.numpy as jnp
from jax import lax
from jax.experimental import pallas as pl
from jax.experimental.pallas import tpu as pltpu
from jax.sharding import PartitionSpec as P

epsilon = 1e-06
code_max = 448.0
outer_rate = 0.7
nesterov = 0.9

BLOCK = 128
GROUP = 16
MESH = pl.DeviceIdType.MESH

LAG_ENCODE = -1
LAG_PAIR = 0
LAG_OWN = 3
LAG_PASS = 6
SLOTS = 4
PARTS = 8
RING = 10


def round_trip(values):
    largest = jnp.max(jnp.abs(values), axis=-1, keepdims=True)
    scales = ((largest + epsilon) / code_max).astype(jnp.bfloat16).astype(jnp.float32)
    symbols = (values * (1.0 / scales)).astype(jnp.bfloat16)
    return symbols.astype(jnp.float32) * scales


def kernel(
    rep_count, fsdp_count, chunk, base, loc, mom, out,
    base_buf, loc_buf, mom_buf, mom_out, sib_out, pair_out, new_out,
    sib_in, pair_in, mom_in,
    base_sem, loc_sem, mom_sem,
    mom_send, sib_send, pair_send, new_send, pass_send,
    sib_recv, pair_recv, mom_recv, new_recv, far_recv, sib_free, pair_free,
):
    r = lax.axis_index("rep")
    f = lax.axis_index("fsdp")
    x = lax.div(r, 2)
    c = lax.rem(r, 2)
    sibling = (2 * x + 1 - c, f)
    across = (2 * (1 - x) + c, f)
    cols = base.shape[1]
    quarter_rows = base.shape[0] // rep_count
    own_rows = mom.shape[0]
    per_piece = own_rows // chunk
    chunks = quarter_rows // chunk
    quarters = (2 * (1 - x) + 1 - c, 2 * x + 1 - c, 2 * (1 - x) + c, 2 * x + c)
    lags = (LAG_ENCODE, LAG_ENCODE, LAG_PAIR, LAG_OWN)

    barrier = pltpu.get_barrier_semaphore()
    pl.semaphore_signal(barrier, inc=1, device_id=sibling, device_id_type=MESH)
    pl.semaphore_signal(barrier, inc=1, device_id=across, device_id_type=MESH)

    def greet(j, carry):
        peer = lax.rem(f + j, fsdp_count)
        pl.semaphore_signal(barrier, inc=1, device_id=(r, peer), device_id_type=MESH)
        return carry

    lax.fori_loop(1, fsdp_count, greet, 0)

    def rows_of(k, quarter):
        piece = lax.rem(f + lax.div(k, per_piece), fsdp_count)
        start = quarter * quarter_rows + piece * own_rows + lax.rem(k, per_piece) * chunk
        return pl.ds(pl.multiple_of(start, 16), chunk)

    def mom_peer(k):
        return lax.rem(f + fsdp_count - lax.div(k, per_piece), fsdp_count)

    def loads(i, k):
        slot = lax.rem(k, 2)
        rows = rows_of(k, quarters[i])
        return (
            pltpu.make_async_copy(base.at[rows, :], base_buf.at[slot, i], base_sem.at[slot, i]),
            pltpu.make_async_copy(loc.at[0, rows, :], loc_buf.at[slot, i], loc_sem.at[slot, i]),
        )

    def mom_load(k):
        slot = lax.rem(k, 2)
        start = pl.multiple_of(lax.rem(k, per_piece) * chunk, 16)
        first = pl.multiple_of(mom_peer(k) * cols, BLOCK)
        return pltpu.make_async_copy(
            mom.at[pl.ds(start, chunk), pl.ds(first, cols)], mom_buf.at[slot], mom_sem.at[slot]
        )

    def remote(src, dst, send, recv, device):
        return pltpu.make_async_remote_copy(
            src_ref=src, dst_ref=dst, send_sem=send, recv_sem=recv,
            device_id=device, device_id_type=MESH,
        )

    def mom_copy(k):
        slot = lax.rem(k, SLOTS)
        return remote(
            mom_out.at[slot], mom_in.at[k], mom_send.at[slot], mom_recv.at[k], (r, mom_peer(k))
        )

    def sib_copy(i, k):
        slot = lax.rem(k, SLOTS)
        return remote(
            sib_out.at[slot, i], sib_in.at[lax.rem(k, RING), i], sib_send.at[slot, i],
            sib_recv.at[lax.rem(k, RING), i], sibling,
        )

    def pair_copy(k):
        slot = lax.rem(k, SLOTS)
        return remote(
            pair_out.at[slot], pair_in.at[lax.rem(k, RING)], pair_send.at[slot],
            pair_recv.at[lax.rem(k, RING)], across,
        )

    def new_copies(k):
        slot = lax.rem(k, SLOTS)
        src = new_out.at[slot]
        dst = out.at[rows_of(k, quarters[3]), :]
        return (
            remote(src, dst, new_send.at[slot, 0], new_recv.at[k], across),
            remote(src, dst, new_send.at[slot, 1], far_recv.at[0], sibling),
            pltpu.make_async_copy(src, dst, new_send.at[slot, 2]),
        )

    def pass_copy(rows):
        return remote(out.at[rows, :], out.at[rows, :], pass_send, far_recv.at[1], sibling)

    def active(k):
        return jnp.logical_and(k >= 0, k < chunks)

    def prefetch(step):
        @pl.when(active(step))
        def _():
            mom_load(step).start()

        for i in range(4):
            k = step - lags[i]

            @pl.when(active(k))
            def _(i=i, k=k):
                for copy in loads(i, k):
                    copy.start()

    def each_block(body):
        def group(g, carry):
            rows = pl.ds(pl.multiple_of(g * GROUP, GROUP), GROUP)
            for b in range(cols // BLOCK):
                body(rows, pl.ds(b * BLOCK, BLOCK))
            return carry

        lax.fori_loop(0, chunk // GROUP, group, 0)

    def change(i, slot, rows, block):
        start = base_buf[slot, i, rows, block].astype(jnp.float32)
        return start, round_trip(start - loc_buf[slot, i, rows, block].astype(jnp.float32))

    def send_momentum(k):
        slot = lax.rem(k, 2)
        mom_load(k).wait()

        @pl.when(k < per_piece)
        def _():
            def body(rows, block):
                mom_in[k, rows, block] = mom_buf[slot, rows, block].astype(jnp.bfloat16)

            each_block(body)

        @pl.when(k >= per_piece)
        def _():
            @pl.when(k >= per_piece + SLOTS)
            def _():
                mom_copy(k - SLOTS).wait_send()

            to = lax.rem(k, SLOTS)

            def body(rows, block):
                mom_out[to, rows, block] = mom_buf[slot, rows, block].astype(jnp.bfloat16)

            each_block(body)
            mom_copy(k).start()

    def send_sibling(k):
        @pl.when(k >= RING)
        def _():
            pl.semaphore_wait(sib_free, 1)

        for i in range(2):
            sib_copy(i, k).start()

    def encode_sibling(k):
        slot = lax.rem(k, 2)
        to = lax.rem(k, SLOTS)
        for i in range(2):
            for copy in loads(i, k):
                copy.wait()

            @pl.when(k >= SLOTS)
            def _(i=i):
                sib_copy(i, k - SLOTS).wait_send()

            def body(rows, block, i=i):
                sib_out[to, i, rows, block] = change(i, slot, rows, block)[1].astype(jnp.bfloat16)

            each_block(body)

    def send_pair(k):
        slot = lax.rem(k, 2)
        to = lax.rem(k, SLOTS)
        for copy in loads(2, k):
            copy.wait()

        @pl.when(k >= SLOTS)
        def _():
            pair_copy(k - SLOTS).wait_send()

        @pl.when(k >= RING)
        def _():
            pl.semaphore_wait(pair_free, 1)

        sib_copy(0, k).wait_recv()

        def body(rows, block):
            total = change(2, slot, rows, block)[1] + sib_in[lax.rem(k, RING), 0, rows, block].astype(jnp.float32)
            pair_out[to, rows, block] = total.astype(jnp.bfloat16)

        each_block(body)
        pair_copy(k).start()

    def step_own(k):
        slot = lax.rem(k, 2)
        to = lax.rem(k, SLOTS)
        for copy in loads(3, k):
            copy.wait()

        @pl.when(k >= SLOTS)
        def _():
            first, second, third = new_copies(k - SLOTS)
            first.wait_send()
            second.wait_send()
            third.wait()

        sib_copy(1, k).wait_recv()

        @pl.when(k >= per_piece)
        def _():
            mom_copy(k).wait_recv()

        pair_copy(k).wait_recv()

        def body(rows, block):
            start, mine = change(3, slot, rows, block)
            total = mine + sib_in[lax.rem(k, RING), 1, rows, block].astype(jnp.float32)
            total = total + pair_in[lax.rem(k, RING), rows, block].astype(jnp.float32)
            outer_grad = total / rep_count
            moment_next = nesterov * mom_in[k, rows, block].astype(jnp.float32) + outer_grad
            update = outer_rate * (outer_grad + nesterov * moment_next)
            new_out[to, rows, block] = (start - round_trip(update)).astype(jnp.bfloat16)

        each_block(body)
        for copy in new_copies(k):
            copy.start()

        @pl.when(k < chunks - RING)
        def _():
            pl.semaphore_signal(sib_free, inc=1, device_id=sibling, device_id_type=MESH)
            pl.semaphore_signal(pair_free, inc=1, device_id=across, device_id_type=MESH)

    def pass_on(k):
        rows = rows_of(k, quarters[2])
        remote(
            out.at[rows, :], out.at[rows, :], pass_send, new_recv.at[k], across
        ).wait_recv()
        pass_copy(rows).start()

    prefetch(jnp.int32(-1))
    prefetch(jnp.int32(0))
    encode_sibling(jnp.int32(0))
    pl.semaphore_wait(barrier, fsdp_count + 1)

    def step(s, carry):
        prefetch(s + 1)
        for lag, stage in (
            (0, send_sibling),
            (LAG_ENCODE, encode_sibling),
            (LAG_PAIR, send_pair),
            (LAG_OWN, step_own),
            (0, send_momentum),
            (LAG_PASS, pass_on),
        ):
            k = s - lag

            @pl.when(active(k))
            def _(stage=stage, k=k):
                stage(k)

        return carry

    lax.fori_loop(0, chunks + LAG_PASS, step, 0)

    def drain(k, carry):
        mom_copy(k).wait_send()
        sib_copy(0, k).wait_send()
        sib_copy(1, k).wait_send()
        pair_copy(k).wait_send()
        first, second, third = new_copies(k)
        first.wait_send()
        second.wait_send()
        third.wait()
        return carry

    lax.fori_loop(chunks - SLOTS, chunks, drain, 0)

    def quarter_of(index):
        return pl.ds(pl.multiple_of(index * quarter_rows, 16), quarter_rows)

    pass_copy(quarter_of(quarters[2])).wait_send()
    for i in range(2):
        rows = quarter_of(quarters[1 - i])
        remote(out.at[rows, :], out.at[rows, :], pass_send, far_recv.at[i], sibling).wait_recv()


def write_kernel(rows, src, dst, sem):
    copies = [
        pltpu.make_async_copy(
            src.at[pl.ds(p * rows, rows), :], dst.at[pl.ds(p * rows, rows), :], sem.at[p]
        )
        for p in range(PARTS)
    ]
    for copy in copies:
        copy.start()
    for copy in copies:
        copy.wait()


def chunk_rows(own_rows):
    for size in (64, 80, 96, 112, 128, 48, 32):
        if own_rows % size == 0:
            return size
    return GROUP


def local(base_params, local_params, momentum):
    rep_count = lax.axis_size("rep")
    fsdp_count = lax.axis_size("fsdp")
    total_rows, cols = base_params.shape
    chunk = chunk_rows(momentum.shape[0])
    chunks = total_rows // rep_count // chunk
    bf16, f32 = jnp.bfloat16, jnp.float32
    dma = pltpu.SemaphoreType.DMA
    anywhere = pl.BlockSpec(memory_space=pl.ANY)
    gathered = pl.pallas_call(
        functools.partial(kernel, rep_count, fsdp_count, chunk),
        out_shape=pltpu.VMEM((total_rows, cols), bf16),
        in_specs=[anywhere] * 3,
        out_specs=anywhere,
        scratch_shapes=[
            pltpu.VMEM((2, 4, chunk, cols), bf16),
            pltpu.VMEM((2, 4, chunk, cols), bf16),
            pltpu.VMEM((2, chunk, cols), f32),
            pltpu.VMEM((SLOTS, chunk, cols), bf16),
            pltpu.VMEM((SLOTS, 2, chunk, cols), bf16),
            pltpu.VMEM((SLOTS, chunk, cols), bf16),
            pltpu.VMEM((SLOTS, chunk, cols), bf16),
            pltpu.VMEM((RING, 2, chunk, cols), bf16),
            pltpu.VMEM((RING, chunk, cols), bf16),
            pltpu.VMEM((chunks, chunk, cols), bf16),
            dma((2, 4)),
            dma((2, 4)),
            dma((2,)),
            dma((SLOTS,)),
            dma((SLOTS, 2)),
            dma((SLOTS,)),
            dma((SLOTS, 3)),
            dma,
            dma((RING, 2)),
            dma((RING,)),
            dma((chunks,)),
            dma((chunks,)),
            dma((2,)),
            pltpu.SemaphoreType.REGULAR,
            pltpu.SemaphoreType.REGULAR,
        ],
        compiler_params=pltpu.CompilerParams(
            collective_id=0, has_side_effects=True, vmem_limit_bytes=24 * 1024 * 1024
        ),
    )(base_params, local_params, momentum)
    return pl.pallas_call(
        functools.partial(write_kernel, total_rows // PARTS),
        out_shape=jax.ShapeDtypeStruct((total_rows, cols), bf16),
        in_specs=[anywhere],
        out_specs=anywhere,
        scratch_shapes=[dma((PARTS,))],
        compiler_params=pltpu.CompilerParams(vmem_limit_bytes=1024 * 1024),
    )(gathered)


def solution(mesh):
    return jax.shard_map(
        local,
        mesh=mesh,
        in_specs=(P(None, "fsdp"), P("rep", None, "fsdp"), P(("rep", "fsdp"), None)),
        out_specs=P(None, "fsdp"),
        check_vma=False,
    )
```
